256 devices in a mesh: occ: 16 (over z_lo, x), aux: 16 (over y, z_hi, core).
Axes of the slice: x: 4, y: 4, z: 8 (z_hi: 2, z_lo: 4; z = z_hi * 4 + z_lo), core: 2. Of those that a mesh axis runs over, the one named last changes fastest.
Arguments:
- factor: bfloat16 [16, 96, 256, 256], P('occ', 'aux'), may hold values from -0.375 to 0.375
- amplitudes: bfloat16 [512, 256, 256], P('occ'), may hold values from -0.625 to 0.625
- pair_domain: int32 [512], P('occ'), may hold values from 0 to 15, as said below
- pair_count: int32 [16], replicated, may hold values from 1 to 32, 256 in all
Outputs:
- ladder: float32 [512, 256, 256], P('occ', 'aux')
The draws below stay inside these ranges and needn't reach their ends.
Inputs may be any that keep to these rules, and one draw needn't show every extreme that they name: `pair_domain`: among the 32 slots of one occupied block at most 3 name one domain block, and some domain block is named by exactly 3 of them in every occupied block. `pair_count`: the largest count equals 32 in every draw.
All inputs are finite; a program needn't handle non-finite values.
Results may differ from the reference program's by a relative error of at most 0.0029.
Values may be sent and summed in bfloat16 or wider, within the bound.
A program may use at most 128 MiB of HBM per device.

```python
import math
import jax
import jax.numpy as jnp
import numpy as np
from jax import lax

VB = 256
CAP = 32
NBLK = 16
NAUX = 96
NPAIR = 512
MOST = 3
N_OCC = 16


def draw_pair_domain(key, part):
    key = jax.random.fold_in(key, 11)

    def one_block(block_key):
        first, second, third = jax.random.split(block_key, 3)
        heavy = jax.random.randint(first, (), 0, NBLK, dtype=jnp.int32)
        others = (NBLK - 1) * MOST
        offsets = jnp.arange(others, dtype=jnp.int32) // MOST
        pool = (heavy + 1 + offsets) % NBLK
        picked = jax.random.permutation(second, pool)[:CAP - MOST]
        filled = jnp.concatenate([picked, jnp.full((MOST,), heavy, dtype=jnp.int32)])
        return jax.random.permutation(third, filled)
    block_keys = jax.random.split(key, N_OCC)
    return jax.vmap(one_block)(block_keys).reshape(NPAIR).astype(jnp.int32)


def level_of(own_key, extent, cuts, low, top_value):
    level = 1.0
    for dim, blocks in cuts:
        steps = jax.random.uniform(jax.random.fold_in(jax.random.fold_in(own_key, 6), dim), (blocks,), jnp.float32, low / len(cuts), top_value / len(cuts))
        level = level * jnp.repeat(jnp.exp(steps), extent[dim] // blocks).reshape((-1,) + (1,) * (len(extent) - 1 - dim))
    return level


def split_up(number_of, total, limit, slope):
    loads = [(1 << 20) // math.isqrt(grade ** slope) + 1 for grade in range(2, number_of + 1)]
    rest, holding = total - limit - (number_of - 1), [1] * (number_of - 1)
    while rest > 0:
        candidates = [i for i in range(number_of - 1) if holding[i] < limit]
        whole, budget = sum([loads[i] for i in candidates]), rest
        for i in candidates:
            addition = min(limit - holding[i], max(1, budget * loads[i] // whole), rest)
            holding[i] = holding[i] + addition
            rest = rest - addition
    return np.array([limit] + holding)


def ragged_sizes(stream_key, amount, total, reach, lean):
    if amount == 2:
        one = jax.random.randint(stream_key, (), max(1, total - reach), min(reach, total - 1) + 1)
        return jnp.stack([one, total - one])
    lengths = jnp.asarray(split_up(amount, total, reach, lean), jnp.int32)
    couples = (amount - 1) // 2
    giver, taker = lengths[1:1 + 2 * couples:2], lengths[2:2 + 2 * couples:2]
    room = jnp.minimum(giver - 1, reach - taker)
    passed = jax.random.randint(jax.random.fold_in(stream_key, 1), (couples,), 0, 1 << 20) % (room + 1)
    lengths = lengths.at[1:1 + 2 * couples:2].set(giver - passed).at[2:2 + 2 * couples:2].set(taker + passed)
    return lengths[jax.random.permutation(jax.random.fold_in(stream_key, 2), amount)]


def scatter_about(key, extent, width, bound, cuts=(), kind=jnp.bfloat16):
    loudness = level_of(key, extent, cuts, -0.22, 0.18) if cuts else 1.0
    array = jax.random.normal(key, extent, jnp.float32) * width * loudness
    return jnp.minimum(jnp.maximum(array, -bound), bound).astype(kind)


def setup_inputs(seed: int = 0) -> dict:
    key_list = jax.random.split(jax.random.key(seed), 5)
    factor = scatter_about(key_list[0], (NBLK, NAUX, VB, VB), VB ** -0.5, 0.375, ((0, 16), (1, 16)))
    amplitudes = scatter_about(key_list[1], (NPAIR, VB, VB), NAUX ** -0.5, 0.625, ((0, 16),))
    pair_domain = draw_pair_domain(jax.random.fold_in(key_list[4], 71), 0)
    pair_count = ragged_sizes(key_list[3], N_OCC, N_OCC * CAP // 2, CAP, 2).astype(jnp.int32)
    return {"factor": factor, "amplitudes": amplitudes, "pair_domain": pair_domain, "pair_count": pair_count}


def reference(factor, amplitudes, pair_domain, pair_count):
    slot_index = jnp.arange(NPAIR, dtype=jnp.int32)
    owner = slot_index // CAP
    live = (slot_index % CAP) < pair_count[owner]

    def one_pair(packed):
        amp, domain, alive = packed

        def compute(unused):
            block = lax.dynamic_index_in_dim(factor, domain.astype(jnp.int32), 0, keepdims=False).astype(jnp.float32)
            half = jnp.einsum("qac,cd->qad", block, amp.astype(jnp.float32)).astype(jnp.bfloat16)
            half = lax.optimization_barrier(half).astype(jnp.float32)
            return jnp.einsum("qad,qbd->ab", half, block)

        def skipped(unused):
            return jnp.zeros((VB, VB), jnp.float32)

        return lax.cond(alive, compute, skipped, 0)

    return lax.map(one_pair, (amplitudes, pair_domain, live))
```

```python
import jax
import jax.numpy as jnp
from jax import lax
from jax.experimental import pallas as pl
from jax.experimental.pallas import tpu as pltpu
from jax.sharding import PartitionSpec as P

MESH = pl.DeviceIdType.MESH
NT = (((1,), (1,)), ((), ()))
NQ = 3
CHUNKS = 16
CAP = 3
ROWS = 16


def kernel(
    factor, amps, domain, count, out,
    fbuf, ampv, packed, arecv, acc, ebuf, erecv, rank,
    fsend, frecv, asend, arecv_sem, esend, erecv_sem, local_sem,
):
    me_o, me_a = lax.axis_index("occ"), lax.axis_index("aux")
    z, x = me_o // 4, me_o % 4
    y, zh, core = me_a // 4, (me_a // 2) % 2, me_a % 2
    up = ((y + 1) % 4) * 4 + me_a % 4
    down = ((y + 3) % 4) * 4 + me_a % 4
    sibling = me_a + 1 - 2 * core

    def shift(j):
        dx = core + 2 * j
        return dx, (dx + y) % 4

    def ahead(j):
        dx, dz = shift(j)
        return ((z + dz) % 4) * 4 + (x + dx) % 4

    def behind(j):
        dx, dz = shift(j)
        return ((z + 4 - dz) % 4) * 4 + (x + 4 - dx) % 4

    def server(i):
        dx, dz, half = i % 4, (i // 4) % 4, i // 16
        src_o = ((z + dz) % 4) * 4 + (x + dx) % 4
        src_a = (((dz + 4 - dx) % 4) * 2 + half) * 2 + dx % 2
        return src_o, src_a, half

    get_factor = pltpu.make_async_copy(factor, fbuf.at[pl.ds(0, 2)], local_sem.at[0])
    get_amps = pltpu.make_async_copy(amps, ampv, local_sem.at[1])
    get_factor.start()
    get_amps.start()

    barrier = pltpu.get_barrier_semaphore()
    for peer in (up, down, sibling):
        pl.semaphore_signal(barrier, inc=1, device_id=(me_o, peer), device_id_type=MESH)
    for j in range(2):
        src = behind(j)

        @pl.when(src != me_o)
        def _():
            pl.semaphore_signal(barrier, inc=1, device_id=(src, me_a), device_id_type=MESH)

    def greet(i, carry):
        src_o, src_a, _ = server(i)

        @pl.when(jnp.logical_or(src_o != me_o, src_a != me_a))
        def _():
            pl.semaphore_signal(barrier, inc=1, device_id=(src_o, src_a), device_id_type=MESH)

        return carry

    lax.fori_loop(0, 32, greet, 0)
    at_home = jnp.where(jnp.logical_and(y == 0, core == 0), 1, 0)

    def find(p, carry):
        own = domain[p]

        def earlier(q, k):
            return k + jnp.where(domain[q] == own, 1, 0)

        rank[p] = lax.fori_loop(0, p, earlier, 0)
        new = []
        for j in range(2):
            seen, picks = carry[j]
            hit = own == ahead(j)
            picks = tuple(jnp.where(jnp.logical_and(hit, seen == k), p, picks[k]) for k in range(CAP))
            new.append((seen + jnp.where(hit, 1, 0), picks))
        return tuple(new)

    zero = jnp.int32(0)
    start = (zero, (zero, zero, zero))
    found = lax.fori_loop(0, 32, find, (start, start))

    pl.semaphore_wait(barrier, 37 - 2 * at_home)

    def fcopy(src, dst, n, peer):
        return pltpu.make_async_remote_copy(
            src_ref=fbuf.at[src], dst_ref=fbuf.at[dst], send_sem=fsend.at[n], recv_sem=frecv.at[dst],
            device_id=(me_o, peer), device_id_type=MESH,
        )

    get_factor.wait()
    sends = [
        fcopy(0, 4, 0, up), fcopy(1, 5, 1, down), fcopy(0, 2, 2, sibling), fcopy(1, 3, 3, sibling),
        fcopy(1, 8, 4, up), fcopy(0, 9, 5, down),
    ]
    for c in sends:
        c.start()
    later = {
        4: [fcopy(4, 12, 6, up), fcopy(4, 6, 7, sibling)],
        5: [fcopy(5, 13, 8, down), fcopy(5, 7, 9, sibling)],
        8: [fcopy(8, 10, 10, sibling)],
        9: [fcopy(9, 11, 11, sibling)],
        12: [fcopy(12, 14, 12, sibling)],
        13: [fcopy(13, 15, 13, sibling)],
    }
    recvd = {dst: fcopy(dst, dst, 0, sibling) for dst in range(2, CHUNKS)}

    def arrive(*chunks):
        for c in chunks:
            recvd[c].wait_recv()
            for more in later.get(c, ()):
                more.start()

    get_amps.wait()

    def acopy(j, k, dst_o):
        s = j * CAP + k
        return pltpu.make_async_remote_copy(
            src_ref=packed.at[s], dst_ref=arecv.at[s], send_sem=asend.at[s], recv_sem=arecv_sem.at[s],
            device_id=(dst_o, me_a), device_id_type=MESH,
        )

    for k in range(CAP):
        for j in range(2):
            s = j * CAP + k
            packed[s] = ampv[found[j][1][k]]
            dst = ahead(j)

            @pl.when(dst != me_o)
            def _():
                acopy(j, k, dst).start()

            @pl.when(dst == me_o)
            def _():
                pltpu.make_async_copy(packed.at[s], arecv.at[s], arecv_sem.at[s]).start()

    def amps_arrive(k):
        for j in range(2):
            acopy(j, k, me_o).wait_recv()

    acc[...] = jnp.zeros(acc.shape, jnp.float32)

    def compute(chunk, slots):
        b = fbuf[chunk]
        tall = b.reshape(NQ * 256, 256)
        wide = jnp.concatenate([b[q] for q in range(NQ)], axis=1)
        for s in slots:
            half = jnp.dot(tall, arecv[s], preferred_element_type=jnp.float32).astype(jnp.bfloat16)
            half = jnp.concatenate([half[q * 256:(q + 1) * 256] for q in range(NQ)], axis=1)
            acc[s] += lax.dot_general(half, wide, NT, preferred_element_type=jnp.float32)

    def compute_run(first, stop, slots):
        def body(i, carry):
            compute(i, slots)
            return carry

        lax.fori_loop(first, stop, body, 0)

    k0, k1, k2 = (0, 3), (1, 4), (2, 5)
    every = (0, 3, 1, 4, 2, 5)
    amps_arrive(0)
    arrive(2, 3)
    compute_run(0, 4, k0)
    arrive(4, 5)
    compute_run(4, 6, k0)
    amps_arrive(1)
    compute_run(0, 6, k1)
    arrive(6, 7)
    compute_run(6, 8, k0 + k1)
    arrive(8, 9)
    compute_run(8, 10, k0 + k1)
    amps_arrive(2)
    compute_run(0, 10, k2)
    arrive(10, 11)
    compute_run(10, 12, every)
    arrive(12, 13)
    compute_run(12, 14, every)
    arrive(14, 15)

    def ecopy(j, a, dst_o):
        n = j * 16 + a
        return pltpu.make_async_remote_copy(
            src_ref=ebuf.at[j, :, pl.ds(pl.multiple_of(a * ROWS, ROWS), ROWS), :],
            dst_ref=erecv.at[zh * 16 + me_o],
            send_sem=esend.at[n], recv_sem=erecv_sem.at[zh * 16 + me_o],
            device_id=(dst_o, a), device_id_type=MESH,
        )

    for j in range(2):
        compute_run(14, 16, tuple(range(j * CAP, (j + 1) * CAP)))
        for k in range(CAP):
            ebuf[j, k] = acc[j * CAP + k].astype(jnp.bfloat16)
        dst_o = behind(j)

        def give(a, carry):
            away = jnp.logical_or(dst_o != me_o, a != me_a)

            @pl.when(away)
            def _():
                ecopy(j, a, dst_o).start()

            @pl.when(jnp.logical_not(away))
            def _():
                pltpu.make_async_copy(
                    ebuf.at[j, :, pl.ds(pl.multiple_of(a * ROWS, ROWS), ROWS), :],
                    erecv.at[zh * 16 + me_o], erecv_sem.at[zh * 16 + me_o],
                ).start()

            return carry

        lax.fori_loop(0, 16, give, 0)

    def take(i, carry):
        pltpu.make_async_copy(erecv.at[i], erecv.at[i], erecv_sem.at[i]).wait()
        return carry

    lax.fori_loop(0, 32, take, 0)

    live = count[me_o]

    def unpack(p, carry):
        d, k = jnp.clip(domain[p], 0, 15), jnp.minimum(rank[p], CAP - 1)
        term = erecv[d, k].astype(jnp.float32) + erecv[16 + d, k].astype(jnp.float32)
        out[p] = jnp.where(p < live, term, 0.0)
        return carry

    lax.fori_loop(0, 32, unpack, 0)

    for c in sends:
        c.wait_send()
    for group in later.values():
        for c in group:
            c.wait_send()
    for j in range(2):
        dst = ahead(j)

        @pl.when(dst != me_o)
        def _():
            for k in range(CAP):
                acopy(j, k, dst).wait_send()

        dst_o = behind(j)

        def sent(a, carry):
            @pl.when(jnp.logical_or(dst_o != me_o, a != me_a))
            def _():
                ecopy(j, a, dst_o).wait_send()

            return carry

        lax.fori_loop(0, 16, sent, 0)


def per_device(factor, amplitudes, pair_domain, pair_count):
    hbm = pl.BlockSpec(memory_space=pl.ANY)
    smem = pl.BlockSpec(memory_space=pltpu.SMEM)
    wide = (256, 256)
    return pl.pallas_call(
        kernel,
        out_shape=jax.ShapeDtypeStruct((32, ROWS, 256), jnp.float32),
        in_specs=[hbm, hbm, smem, smem],
        out_specs=pl.BlockSpec(memory_space=pltpu.VMEM),
        scratch_shapes=[
            pltpu.VMEM((CHUNKS, NQ) + wide, jnp.bfloat16),
            pltpu.VMEM((32,) + wide, jnp.bfloat16),
            pltpu.VMEM((2 * CAP,) + wide, jnp.bfloat16),
            pltpu.VMEM((2 * CAP,) + wide, jnp.bfloat16),
            pltpu.VMEM((2 * CAP,) + wide, jnp.float32),
            pltpu.VMEM((2, CAP) + wide, jnp.bfloat16),
            pltpu.VMEM((32, CAP, ROWS, 256), jnp.bfloat16),
            pltpu.SMEM((32,), jnp.int32),
            pltpu.SemaphoreType.DMA((14,)),
            pltpu.SemaphoreType.DMA((CHUNKS,)),
            pltpu.SemaphoreType.DMA((2 * CAP,)),
            pltpu.SemaphoreType.DMA((2 * CAP,)),
            pltpu.SemaphoreType.DMA((32,)),
            pltpu.SemaphoreType.DMA((32,)),
            pltpu.SemaphoreType.DMA((2,)),
        ],
        compiler_params=pltpu.CompilerParams(
            collective_id=0, has_side_effects=True, vmem_limit_bytes=48 * 2**20
        ),
        cost_estimate=pl.CostEstimate(flops=20 * 10**9, bytes_accessed=6 * 10**6, transcendentals=0),
    )(factor.reshape(2, NQ, 256, 256), amplitudes, pair_domain, pair_count)


def solution(mesh):
    placed = (P("occ", "aux", None, None), P("occ", None, None), P("occ"), P())
    return jax.shard_map(
        per_device, mesh=mesh, in_specs=placed, out_specs=P("occ", "aux", None), check_vma=False
    )
```

```python
import jax
import jax.numpy as jnp
from jax import lax
from jax.experimental import pallas as pl
from jax.experimental.pallas import tpu as pltpu
from jax.sharding import PartitionSpec as P

MESH = pl.DeviceIdType.MESH
NT = (((1,), (1,)), ((), ()))
CAP = 3
SLOTS = 2 * CAP
ROWS = 16


def kernel(
    factor, amps, domain_hbm, count_hbm, out,
    fbuf, ampv, packed, arecv, acc, ebuf, erecv, domain, count, rank,
    fsend, frecv, asend, arecv_sem, esend, erecv_sem, local_sem, ready,
):
    me_o, me_a = lax.axis_index("occ"), lax.axis_index("aux")
    z, x = me_o // 4, me_o % 4
    y, zh, core = me_a // 4, (me_a // 2) % 2, me_a % 2
    up = ((y + 1) % 4) * 4 + me_a % 4
    down = ((y + 3) % 4) * 4 + me_a % 4
    sibling = me_a + 1 - 2 * core
    partner = me_a + 2 - 4 * zh
    z8 = zh * 4 + z

    def steps(j):
        dx = core + 2 * j
        dz = (dx + y) % 4
        return dx, dz, jnp.where(dz == 3, 7, dz)

    def ahead(j):
        dx, _, ring = steps(j)
        to = (z8 + ring) % 8
        return (to % 4) * 4 + (x + dx) % 4, (y * 2 + to // 4) * 2 + core

    def behind(j):
        dx, _, ring = steps(j)
        to = (z8 + 8 - ring) % 8
        return (to % 4) * 4 + (x + 4 - dx) % 4, (y * 2 + to // 4) * 2 + core

    get_factor = pltpu.make_async_copy(factor, fbuf.at[pl.ds(0, 6)], local_sem.at[0])
    get_amps = pltpu.make_async_copy(amps, ampv, local_sem.at[1])
    get_domain = pltpu.make_async_copy(domain_hbm, domain, local_sem.at[2])
    get_count = pltpu.make_async_copy(count_hbm, count, local_sem.at[3])
    get_domain.start()
    get_factor.start()
    get_amps.start()
    get_count.start()

    barrier = pltpu.get_barrier_semaphore()
    for peer in (up, down, sibling, partner):
        pl.semaphore_signal(barrier, inc=1, device_id=(me_o, peer), device_id_type=MESH)
    targets = [ahead(j) for j in range(2)]
    origins = [behind(j) for j in range(2)]
    for j in range(2):
        src = origins[j]

        @pl.when(src[0] != me_o)
        def _():
            pl.semaphore_signal(barrier, inc=1, device_id=src, device_id_type=MESH)

    def find(p, carry):
        own = domain[p]
        new = []
        for j in range(2):
            seen, picks = carry[j]
            hit = own == targets[j][0]
            picks = tuple(jnp.where(jnp.logical_and(hit, seen == k), p, picks[k]) for k in range(CAP))
            new.append((seen + jnp.where(hit, 1, 0), picks))
        return tuple(new)

    get_domain.wait()
    zero = jnp.int32(0)
    start = (zero, (zero, zero, zero))
    found = lax.fori_loop(0, 32, find, (start, start))

    at_home = jnp.where(jnp.logical_and(y == 0, core == 0), 1, 0)
    pl.semaphore_wait(barrier, 6 - at_home)

    def fcopy(src, dst, size, n, peer):
        return pltpu.make_async_remote_copy(
            src_ref=fbuf.at[pl.ds(src, size)], dst_ref=fbuf.at[pl.ds(dst, size)],
            send_sem=fsend, recv_sem=frecv.at[n], device_id=(me_o, peer), device_id_type=MESH,
        )

    def arrived(first, size, n):
        ref = fbuf.at[pl.ds(first, size)]
        pltpu.make_async_copy(ref, ref, frecv.at[n]).wait()

    get_factor.wait()
    fcopy(0, 12, 3, 0, up).start()
    fcopy(3, 15, 3, 0, down).start()
    fcopy(0, 6, 6, 1, sibling).start()
    get_amps.wait()

    def amps_go(k):
        for j in range(2):
            src, dst = packed.at[j, k], arecv.at[2 * k + j]
            packed[j, k] = ampv[found[j][1][k]]

            @pl.when(targets[j][0] != me_o)
            def _():
                pltpu.make_async_remote_copy(
                    src_ref=src, dst_ref=dst, send_sem=asend.at[j], recv_sem=arecv_sem.at[k],
                    device_id=targets[j], device_id_type=MESH,
                ).start()

            @pl.when(targets[j][0] == me_o)
            def _():
                pltpu.make_async_copy(src, dst, arecv_sem.at[k]).start()

    def amps_arrive(k):
        ref = arecv.at[pl.ds(2 * k, 2)]
        pltpu.make_async_copy(ref, ref, arecv_sem.at[k]).wait()

    for k in range(CAP):
        amps_go(k)
    fcopy(3, 24, 3, 2, up).start()
    fcopy(0, 27, 3, 2, down).start()

    def tell(n, device):
        pl.semaphore_signal(ready.at[n], inc=1, device_id=device, device_id_type=MESH)

    def hear(n):
        pl.semaphore_wait(ready.at[n], 1)

    tell(0, (me_o, sibling))

    def place(p, carry):
        own = domain[p]
        before = zero
        for q in range(31):
            before += jnp.where(jnp.logical_and(domain[q] == own, q < p), 1, 0)
        rank[p] = before
        return carry

    lax.fori_loop(0, 32, place, 0)
    get_count.wait()
    acc[...] = jnp.zeros(acc.shape, jnp.float32)

    def compute(first, size, slots):
        b = fbuf[pl.ds(first, size)]
        tall = b.reshape(size * 256, 256)
        wide = jnp.concatenate([b[q] for q in range(size)], axis=1)
        for s in slots:
            half = jnp.dot(tall, arecv[s], preferred_element_type=jnp.float32).astype(jnp.bfloat16)
            half = jnp.concatenate([half[q * 256:(q + 1) * 256] for q in range(size)], axis=1)
            acc[s] += lax.dot_general(half, wide, NT, preferred_element_type=jnp.float32)

    hear(0)
    tell(1, (me_o, partner))

    def places(first, stop, k):
        def body(i, carry):
            compute(6 * i, 6, (2 * k, 2 * k + 1))
            return carry

        lax.fori_loop(first, stop, body, 0)

    def ranks(place):
        def body(k, carry):
            compute(6 * place, 6, (2 * k, 2 * k + 1))
            return carry

        lax.fori_loop(0, 2, body, 0)

    arrived(6, 6, 1)
    amps_arrive(0)
    places(0, 2, 0)
    amps_arrive(1)
    places(0, 2, 1)
    arrived(12, 6, 0)
    for g in range(3):
        fcopy(12 + g, 36 + 4 * g, 1, 3 + g, up).start()
        fcopy(15 + g, 37 + 4 * g, 1, 3 + g, down).start()
    fcopy(12, 18, 6, 6, sibling).start()
    hear(1)
    tell(2, (me_o, up))
    tell(3, (me_o, down))
    ranks(2)
    arrived(18, 6, 6)
    ranks(3)
    amps_arrive(2)
    hear(2)
    hear(3)
    tell(4, (me_o, up))
    places(0, 4, 2)
    hear(4)
    for j in range(2):
        @pl.when(targets[j][0] != me_o)
        def _():
            tell(5 + j, targets[j])

    def relay(g):
        arrived(36 + 4 * g, 2, 3 + g)
        fcopy(36 + 4 * g, 38 + 4 * g, 2, 8 + g, sibling).start()

    arrived(24, 6, 2)
    fcopy(24, 30, 6, 7, sibling).start()
    compute(24, 6, range(SLOTS))
    relay(0)
    arrived(30, 6, 7)
    compute(30, 6, range(SLOTS))
    for g in range(2):
        relay(g + 1)
        arrived(38 + 4 * g, 2, 8 + g)
        compute(36 + 4 * g, 4, range(SLOTS))
    for j in range(2):
        @pl.when(origins[j][0] != me_o)
        def _():
            hear(5 + j)
    arrived(46, 2, 10)

    place_here = zh * 16 + me_o
    for j in range(2):
        compute(44, 4, range(j, SLOTS, 2))
        for k in range(CAP):
            ebuf[j, k] = acc[2 * k + j].astype(jnp.bfloat16)
        home = origins[j][0] == me_o

        def give(i, carry):
            a = (me_a + i) % 16
            src = ebuf.at[j, :, pl.ds(pl.multiple_of(a * ROWS, ROWS), ROWS), :]
            here = jnp.logical_and(home, i == 0)

            @pl.when(jnp.logical_not(here))
            def _():
                pltpu.make_async_remote_copy(
                    src_ref=src, dst_ref=erecv.at[place_here], send_sem=esend.at[j], recv_sem=erecv_sem,
                    device_id=(origins[j][0], a), device_id_type=MESH,
                ).start()

            @pl.when(here)
            def _():
                pltpu.make_async_copy(src, erecv.at[place_here], erecv_sem).start()

            return carry

        lax.fori_loop(0, 16, give, 0)

    def sent(ref, sem):
        pltpu.make_async_copy(ref, ref, sem).wait()

    sent(fbuf.at[pl.ds(0, 42)], fsend)
    for j in range(2):
        @pl.when(targets[j][0] != me_o)
        def _():
            sent(packed.at[j], asend.at[j])

    pltpu.make_async_copy(erecv, erecv, erecv_sem).wait()

    live = count[me_o]

    def unpack(p, carry):
        d, k = jnp.clip(domain[p], 0, 15), jnp.minimum(rank[p], CAP - 1)
        term = erecv[d, k].astype(jnp.float32) + erecv[16 + d, k].astype(jnp.float32)
        out[p] = jnp.where(p < live, term, 0.0)
        return carry

    lax.fori_loop(0, 32, unpack, 0)

    for j in range(2):
        @pl.when(origins[j][0] != me_o)
        def _():
            sent(ebuf.at[j], esend.at[j])

        @pl.when(origins[j][0] == me_o)
        def _():
            sent(ebuf.at[j, :, pl.ds(0, 15 * ROWS), :], esend.at[j])


def per_device(factor, amplitudes, pair_domain, pair_count):
    hbm = pl.BlockSpec(memory_space=pl.ANY)
    square = (256, 256)
    return pl.pallas_call(
        kernel,
        out_shape=jax.ShapeDtypeStruct((32, ROWS, 256), jnp.float32),
        in_specs=[hbm, hbm, hbm, hbm],
        out_specs=pl.BlockSpec(memory_space=pltpu.VMEM),
        scratch_shapes=[
            pltpu.VMEM((48,) + square, jnp.bfloat16),
            pltpu.VMEM((32,) + square, jnp.bfloat16),
            pltpu.VMEM((2, CAP) + square, jnp.bfloat16),
            pltpu.VMEM((SLOTS,) + square, jnp.bfloat16),
            pltpu.VMEM((SLOTS,) + square, jnp.float32),
            pltpu.VMEM((2, CAP) + square, jnp.bfloat16),
            pltpu.VMEM((32, CAP, ROWS, 256), jnp.bfloat16),
            pltpu.SMEM((32,), jnp.int32),
            pltpu.SMEM((16,), jnp.int32),
            pltpu.SMEM((32,), jnp.int32),
            pltpu.SemaphoreType.DMA,
            pltpu.SemaphoreType.DMA((11,)),
            pltpu.SemaphoreType.DMA((2,)),
            pltpu.SemaphoreType.DMA((CAP,)),
            pltpu.SemaphoreType.DMA((2,)),
            pltpu.SemaphoreType.DMA,
            pltpu.SemaphoreType.DMA((4,)),
            pltpu.SemaphoreType.REGULAR((7,)),
        ],
        compiler_params=pltpu.CompilerParams(
            collective_id=0, has_side_effects=True, vmem_limit_bytes=64 * 2**20 - 2**16
        ),
        cost_estimate=pl.CostEstimate(flops=20 * 10**9, bytes_accessed=6 * 10**6, transcendentals=0),
    )(factor.reshape(6, 256, 256), amplitudes, pair_domain, pair_count)


def solution(mesh):
    placed = (P("occ", "aux", None, None), P("occ", None, None), P("occ"), P())
    return jax.shard_map(
        per_device, mesh=mesh, in_specs=placed, out_specs=P("occ", "aux", None), check_vma=False
    )
```

```python
import jax
import jax.numpy as jnp
from jax import lax
from jax.experimental import pallas as pl
from jax.experimental.pallas import tpu as pltpu
from jax.sharding import PartitionSpec as P

MESH = pl.DeviceIdType.MESH
NT = (((1,), (1,)), ((), ()))
CAP = 3
SLOTS = 2 * CAP
ROWS = 16


def kernel(
    factor, amps, domain_hbm, count_hbm, out,
    fbuf, ampv, packed, arecv, acc, ebuf, erecv, domain, count, rank,
    fsend, frecv, asend, arecv_sem, esend, erecv_sem, local_sem, ready,
):
    me_o, me_a = lax.axis_index("occ"), lax.axis_index("aux")
    z, x = me_o // 4, me_o % 4
    y, zh, core = me_a // 4, (me_a // 2) % 2, me_a % 2
    up = ((y + 1) % 4) * 4 + me_a % 4
    down = ((y + 3) % 4) * 4 + me_a % 4
    sibling = me_a + 1 - 2 * core
    partner = me_a + 2 - 4 * zh
    z8 = zh * 4 + z

    def steps(j, h=0):
        dz = 1 - j + 2 * core
        ring = dz * (1 + 2 * h) if j else dz + 4 * core
        return (dz + 4 - y) % 4, ring

    def ahead(j, h=0):
        dx, ring = steps(j, h)
        to = (z8 + ring) % 8
        return (to % 4) * 4 + (x + dx) % 4, (y * 2 + to // 4) * 2 + core

    def behind(j, h=0):
        dx, ring = steps(j, h)
        to = (z8 + 8 - ring) % 8
        return (to % 4) * 4 + (x + 4 - dx) % 4, (y * 2 + to // 4) * 2 + core

    get_factor = pltpu.make_async_copy(factor, fbuf.at[pl.ds(0, 6)], local_sem.at[0])
    get_amps = pltpu.make_async_copy(amps, ampv, local_sem.at[1])
    get_domain = pltpu.make_async_copy(domain_hbm, domain, local_sem.at[2])
    get_count = pltpu.make_async_copy(count_hbm, count, local_sem.at[3])
    get_domain.start()
    get_factor.start()
    get_amps.start()
    get_count.start()

    barrier = pltpu.get_barrier_semaphore()
    for peer in (up, down, sibling, partner):
        pl.semaphore_signal(barrier, inc=1, device_id=(me_o, peer), device_id_type=MESH)
    targets = [ahead(j) for j in range(2)]
    origins = [behind(j) for j in range(2)]
    for j in range(2):
        src = origins[j]

        @pl.when(src[0] != me_o)
        def _():
            pl.semaphore_signal(barrier, inc=1, device_id=src, device_id_type=MESH)

    @pl.when(core == 1)
    def _():
        pl.semaphore_signal(barrier, inc=1, device_id=behind(1, 1), device_id_type=MESH)

    at_home = jnp.where(jnp.logical_and(y == 0, core == 0), 1, 0)
    pl.semaphore_wait(barrier, 6 + core - at_home)

    def fcopy(src, dst, size, n, peer):
        return pltpu.make_async_remote_copy(
            src_ref=fbuf.at[pl.ds(src, size)], dst_ref=fbuf.at[pl.ds(dst, size)],
            send_sem=fsend, recv_sem=frecv.at[n], device_id=(me_o, peer), device_id_type=MESH,
        )

    def arrived(first, size, n):
        ref = fbuf.at[pl.ds(first, size)]
        pltpu.make_async_copy(ref, ref, frecv.at[n]).wait()

    get_factor.wait()
    fcopy(0, 12, 3, 0, up).start()
    fcopy(3, 15, 3, 0, down).start()
    fcopy(0, 6, 6, 1, sibling).start()

    def find(p, carry):
        own = domain[p]
        new = []
        for j in range(2):
            seen, picks = carry[j]
            hit = own == targets[j][0]
            picks = tuple(jnp.where(jnp.logical_and(hit, seen == k), p, picks[k]) for k in range(CAP))
            new.append((seen + jnp.where(hit, 1, 0), picks))
        return tuple(new)

    get_domain.wait()
    zero = jnp.int32(0)
    start = (zero, (zero, zero, zero))
    found = lax.fori_loop(0, 32, find, (start, start))
    get_amps.wait()

    for j in range(2):
        for k in range(CAP):
            packed[j, k] = ampv[found[j][1][k]]

    def amps_go(j):
        for k in range(CAP):
            for h in range(2):
                half = pl.ds(128 * h, 128)
                src, dst = packed.at[j, k, half, :], arecv.at[j * CAP + k, half, :]

                @pl.when(targets[j][0] != me_o)
                def _():
                    pltpu.make_async_remote_copy(
                        src_ref=src, dst_ref=dst, send_sem=asend.at[j], recv_sem=arecv_sem.at[j],
                        device_id=ahead(j, h), device_id_type=MESH,
                    ).start()

                @pl.when(targets[j][0] == me_o)
                def _():
                    pltpu.make_async_copy(src, dst, arecv_sem.at[j]).start()

    amps_go(0)
    fcopy(3, 24, 3, 2, up).start()
    fcopy(0, 27, 3, 2, down).start()

    def amps_arrive(j):
        ref = arecv.at[pl.ds(j * CAP, CAP)]
        pltpu.make_async_copy(ref, ref, arecv_sem.at[j]).wait()

    def tell(n, device):
        pl.semaphore_signal(ready.at[n], inc=1, device_id=device, device_id_type=MESH)

    def hear(n):
        pl.semaphore_wait(ready.at[n], 1)

    tell(0, (me_o, sibling))

    def place(p, carry):
        own = domain[p]
        before = zero
        for q in range(31):
            before += jnp.where(jnp.logical_and(domain[q] == own, q < p), 1, 0)
        rank[p] = before
        return carry

    lax.fori_loop(0, 32, place, 0)
    get_count.wait()
    acc[...] = jnp.zeros(acc.shape, jnp.float32)

    def compute(j, first, size):
        b = fbuf[pl.ds(first, size)]
        tall = b.reshape(size * 256, 256)
        wide = jnp.concatenate([b[q] for q in range(size)], axis=1)
        for s in range(j * CAP, (j + 1) * CAP):
            half = jnp.dot(tall, arecv[s], preferred_element_type=jnp.float32).astype(jnp.bfloat16)
            half = jnp.concatenate([half[q * 256:(q + 1) * 256] for q in range(size)], axis=1)
            acc[s] += lax.dot_general(half, wide, NT, preferred_element_type=jnp.float32)

    def sixes(j, first, stop):
        def body(i, carry):
            compute(j, 6 * i, 6)
            return carry

        lax.fori_loop(first, stop, body, 0)

    def relay(g):
        arrived(36 + 4 * g, 2, 3 + g)
        fcopy(36 + 4 * g, 38 + 4 * g, 2, 8 + g, sibling).start()

    arrived(6, 6, 1)
    amps_arrive(0)
    amps_go(1)
    sixes(0, 0, 2)
    arrived(12, 6, 0)
    for g in range(3):
        fcopy(12 + g, 36 + 4 * g, 1, 3 + g, up).start()
        fcopy(15 + g, 37 + 4 * g, 1, 3 + g, down).start()
    fcopy(12, 18, 6, 6, sibling).start()
    hear(0)
    tell(1, (me_o, partner))
    sixes(0, 2, 3)
    hear(1)
    tell(2, (me_o, up))
    tell(3, (me_o, down))
    arrived(18, 6, 6)
    sixes(0, 3, 4)
    amps_arrive(1)
    hear(2)
    hear(3)
    tell(4, (me_o, up))
    sixes(1, 0, 2)
    hear(4)
    for j in range(2):
        @pl.when(targets[j][0] != me_o)
        def _():
            tell(5 + j, targets[j])

    arrived(24, 6, 2)
    fcopy(24, 30, 6, 7, sibling).start()
    sixes(0, 4, 5)
    arrived(30, 6, 7)
    sixes(0, 5, 6)
    relay(0)
    sixes(1, 2, 3)
    arrived(38, 2, 8)
    compute(0, 36, 4)
    relay(1)
    sixes(1, 3, 4)
    arrived(42, 2, 9)
    compute(0, 40, 4)
    relay(2)
    compute(0, 44, 2)
    sixes(1, 4, 5)
    for j in range(2):
        @pl.when(origins[j][0] != me_o)
        def _():
            hear(5 + j)
    arrived(46, 2, 10)
    compute(0, 46, 2)

    place_here = zh * 16 + me_o
    for j in range(2):
        if j == 1:
            sixes(1, 5, 8)
        for k in range(CAP):
            ebuf[j, k] = acc[j * CAP + k].astype(jnp.bfloat16)
        home = origins[j][0] == me_o

        def give(i, carry):
            a = (me_a + i) % 16
            src = ebuf.at[j, :, pl.ds(pl.multiple_of(a * ROWS, ROWS), ROWS), :]
            here = jnp.logical_and(home, i == 0)

            @pl.when(jnp.logical_not(here))
            def _():
                pltpu.make_async_remote_copy(
                    src_ref=src, dst_ref=erecv.at[place_here], send_sem=esend.at[j], recv_sem=erecv_sem,
                    device_id=(origins[j][0], a), device_id_type=MESH,
                ).start()

            @pl.when(here)
            def _():
                pltpu.make_async_copy(src, erecv.at[place_here], erecv_sem).start()

            return carry

        lax.fori_loop(0, 16, give, 0)

    def sent(ref, sem):
        pltpu.make_async_copy(ref, ref, sem).wait()

    sent(fbuf.at[pl.ds(0, 42)], fsend)
    for j in range(2):
        @pl.when(targets[j][0] != me_o)
        def _():
            sent(packed.at[j], asend.at[j])

    pltpu.make_async_copy(erecv, erecv, erecv_sem).wait()

    live = count[me_o]

    def unpack(p, carry):
        d, k = jnp.clip(domain[p], 0, 15), jnp.minimum(rank[p], CAP - 1)
        term = erecv[d, k].astype(jnp.float32) + erecv[16 + d, k].astype(jnp.float32)
        out[p] = jnp.where(p < live, term, 0.0)
        return carry

    lax.fori_loop(0, 32, unpack, 0)

    for j in range(2):
        @pl.when(origins[j][0] != me_o)
        def _():
            sent(ebuf.at[j], esend.at[j])

        @pl.when(origins[j][0] == me_o)
        def _():
            sent(ebuf.at[j, :, pl.ds(0, 15 * ROWS), :], esend.at[j])


def per_device(factor, amplitudes, pair_domain, pair_count):
    hbm = pl.BlockSpec(memory_space=pl.ANY)
    square = (256, 256)
    return pl.pallas_call(
        kernel,
        out_shape=jax.ShapeDtypeStruct((32, ROWS, 256), jnp.float32),
        in_specs=[hbm, hbm, hbm, hbm],
        out_specs=pl.BlockSpec(memory_space=pltpu.VMEM),
        scratch_shapes=[
            pltpu.VMEM((48,) + square, jnp.bfloat16),
            pltpu.VMEM((32,) + square, jnp.bfloat16),
            pltpu.VMEM((2, CAP) + square, jnp.bfloat16),
            pltpu.VMEM((SLOTS,) + square, jnp.bfloat16),
            pltpu.VMEM((SLOTS,) + square, jnp.float32),
            pltpu.VMEM((2, CAP) + square, jnp.bfloat16),
            pltpu.VMEM((32, CAP, ROWS, 256), jnp.bfloat16),
            pltpu.SMEM((32,), jnp.int32),
            pltpu.SMEM((16,), jnp.int32),
            pltpu.SMEM((32,), jnp.int32),
            pltpu.SemaphoreType.DMA,
            pltpu.SemaphoreType.DMA((11,)),
            pltpu.SemaphoreType.DMA((2,)),
            pltpu.SemaphoreType.DMA((2,)),
            pltpu.SemaphoreType.DMA((2,)),
            pltpu.SemaphoreType.DMA,
            pltpu.SemaphoreType.DMA((4,)),
            pltpu.SemaphoreType.REGULAR((7,)),
        ],
        compiler_params=pltpu.CompilerParams(
            collective_id=0, has_side_effects=True, vmem_limit_bytes=64 * 2**20 - 2**16
        ),
        cost_estimate=pl.CostEstimate(flops=20 * 10**9, bytes_accessed=6 * 10**6, transcendentals=0),
    )(factor.reshape(6, 256, 256), amplitudes, pair_domain, pair_count)


def solution(mesh):
    placed = (P("occ", "aux", None, None), P("occ", None, None), P("occ"), P())
    return jax.shard_map(
        per_device, mesh=mesh, in_specs=placed, out_specs=P("occ", "aux", None), check_vma=False
    )
```

```python
import jax
import jax.numpy as jnp
from jax import lax
from jax.experimental import pallas as pl
from jax.experimental.pallas import tpu as pltpu
from jax.sharding import PartitionSpec as P

MESH = pl.DeviceIdType.MESH
NT = (((1,), (1,)), ((), ()))
CAP = 3
SLOTS = 2 * CAP
ROWS = 16


def kernel(
    factor, amps, domain_hbm, count_hbm, out,
    fbuf, ampv, packed, arecv, acc, ebuf, erecv, domain, count, rank,
    fsend, frecv, asend, arecv_sem, esend, erecv_sem, local_sem, ready,
):
    me_o, me_a = lax.axis_index("occ"), lax.axis_index("aux")
    z, x = me_o // 4, me_o % 4
    y, zh, core = me_a // 4, (me_a // 2) % 2, me_a % 2
    up = ((y + 1) % 4) * 4 + me_a % 4
    down = ((y + 3) % 4) * 4 + me_a % 4
    sibling = me_a + 1 - 2 * core
    partner = me_a + 2 - 4 * zh
    z8 = zh * 4 + z

    def steps(j, h=0):
        dz = 1 - j + 2 * core
        ring = dz * (1 + 2 * h) if j else dz + 4 * core
        return (dz + 4 - y) % 4, ring

    def ahead(j, h=0):
        dx, ring = steps(j, h)
        to = (z8 + ring) % 8
        return (to % 4) * 4 + (x + dx) % 4, (y * 2 + to // 4) * 2 + core

    def behind(j, h=0):
        dx, ring = steps(j, h)
        to = (z8 + 8 - ring) % 8
        return (to % 4) * 4 + (x + 4 - dx) % 4, (y * 2 + to // 4) * 2 + core

    get_factor = pltpu.make_async_copy(factor, fbuf.at[pl.ds(0, 6)], local_sem.at[0])
    get_amps = pltpu.make_async_copy(amps, ampv, local_sem.at[1])
    get_domain = pltpu.make_async_copy(domain_hbm, domain, local_sem.at[2])
    get_count = pltpu.make_async_copy(count_hbm, count, local_sem.at[3])
    get_domain.start()
    get_factor.start()
    get_amps.start()
    get_count.start()

    barrier = pltpu.get_barrier_semaphore()
    for peer in (up, down, sibling, partner):
        pl.semaphore_signal(barrier, inc=1, device_id=(me_o, peer), device_id_type=MESH)
    targets = [ahead(j) for j in range(2)]
    origins = [behind(j) for j in range(2)]
    for j in range(2):
        src = origins[j]

        @pl.when(src[0] != me_o)
        def _():
            pl.semaphore_signal(barrier, inc=1, device_id=src, device_id_type=MESH)

    @pl.when(core == 1)
    def _():
        pl.semaphore_signal(barrier, inc=1, device_id=behind(1, 1), device_id_type=MESH)

    at_home = jnp.where(jnp.logical_and(y == 0, core == 0), 1, 0)
    pl.semaphore_wait(barrier, 6 + core - at_home)

    def fcopy(src, dst, size, n, peer):
        return pltpu.make_async_remote_copy(
            src_ref=fbuf.at[pl.ds(src, size)], dst_ref=fbuf.at[pl.ds(dst, size)],
            send_sem=fsend, recv_sem=frecv.at[n], device_id=(me_o, peer), device_id_type=MESH,
        )

    def arrived(first, size, n):
        ref = fbuf.at[pl.ds(first, size)]
        pltpu.make_async_copy(ref, ref, frecv.at[n]).wait()

    get_factor.wait()
    fcopy(0, 12, 3, 0, up).start()
    fcopy(3, 15, 3, 0, down).start()
    fcopy(0, 6, 6, 1, sibling).start()

    def find(p, carry):
        own = domain[p]
        new = []
        for j in range(2):
            seen, picks = carry[j]
            hit = own == targets[j][0]
            picks = tuple(jnp.where(jnp.logical_and(hit, seen == k), p, picks[k]) for k in range(CAP))
            new.append((seen + jnp.where(hit, 1, 0), picks))
        return tuple(new)

    get_domain.wait()
    zero = jnp.int32(0)
    start = (zero, (zero, zero, zero))
    found = lax.fori_loop(0, 32, find, (start, start))
    get_amps.wait()

    def pack(j):
        for k in range(CAP):
            packed[j, k] = ampv[found[j][1][k]]

    def amps_go(j):
        for k in range(CAP):
            for h in range(2):
                half = pl.ds(128 * h, 128)
                src, dst = packed.at[j, k, half, :], arecv.at[j * CAP + k, half, :]

                @pl.when(targets[j][0] != me_o)
                def _():
                    pltpu.make_async_remote_copy(
                        src_ref=src, dst_ref=dst, send_sem=asend.at[j], recv_sem=arecv_sem.at[j],
                        device_id=ahead(j, h), device_id_type=MESH,
                    ).start()

                @pl.when(targets[j][0] == me_o)
                def _():
                    pltpu.make_async_copy(src, dst, arecv_sem.at[j]).start()

    pack(0)
    amps_go(0)
    pack(1)
    fcopy(3, 24, 3, 2, up).start()
    fcopy(0, 27, 3, 2, down).start()

    def amps_arrive(j):
        ref = arecv.at[pl.ds(j * CAP, CAP)]
        pltpu.make_async_copy(ref, ref, arecv_sem.at[j]).wait()

    def tell(n, device):
        pl.semaphore_signal(ready.at[n], inc=1, device_id=device, device_id_type=MESH)

    def hear(n):
        pl.semaphore_wait(ready.at[n], 1)

    tell(0, (me_o, sibling))

    def place(p, carry):
        own = domain[p]
        before = zero
        for q in range(31):
            before += jnp.where(jnp.logical_and(domain[q] == own, q < p), 1, 0)
        rank[p] = before
        return carry

    lax.fori_loop(0, 32, place, 0)
    get_count.wait()
    hear(0)
    tell(1, (me_o, partner))
    acc[...] = jnp.zeros(acc.shape, jnp.float32)
    hear(1)
    tell(2, (me_o, up))
    tell(3, (me_o, down))

    def compute(j, first, size):
        b = fbuf[pl.ds(first, size)]
        tall = b.reshape(size * 256, 256)
        wide = jnp.concatenate([b[q] for q in range(size)], axis=1)
        for s in range(j * CAP, (j + 1) * CAP):
            half = jnp.dot(tall, arecv[s], preferred_element_type=jnp.float32).astype(jnp.bfloat16)
            half = jnp.concatenate([half[q * 256:(q + 1) * 256] for q in range(size)], axis=1)
            acc[s] += lax.dot_general(half, wide, NT, preferred_element_type=jnp.float32)

    def sixes(j, first, stop):
        def body(i, carry):
            compute(j, 6 * i, 6)
            return carry

        lax.fori_loop(first, stop, body, 0)

    def relay(g):
        arrived(36 + 4 * g, 2, 3 + g)
        fcopy(36 + 4 * g, 38 + 4 * g, 2, 8 + g, sibling).start()

    arrived(6, 6, 1)
    amps_arrive(0)
    amps_go(1)
    sixes(0, 0, 2)
    arrived(12, 6, 0)
    for g in range(3):
        fcopy(12 + g, 36 + 4 * g, 1, 3 + g, up).start()
        fcopy(15 + g, 37 + 4 * g, 1, 3 + g, down).start()
    fcopy(12, 18, 6, 6, sibling).start()
    hear(2)
    hear(3)
    tell(4, (me_o, up))
    sixes(0, 2, 3)
    arrived(18, 6, 6)
    sixes(0, 3, 4)
    hear(4)
    for j in range(2):
        @pl.when(targets[j][0] != me_o)
        def _():
            tell(5 + j, targets[j])

    amps_arrive(1)
    sixes(1, 0, 2)
    arrived(24, 6, 2)
    fcopy(24, 30, 6, 7, sibling).start()
    sixes(0, 4, 5)
    arrived(30, 6, 7)
    sixes(0, 5, 6)
    relay(0)
    sixes(1, 2, 3)
    arrived(38, 2, 8)
    compute(0, 36, 4)
    relay(1)
    arrived(42, 2, 9)
    compute(0, 40, 4)
    relay(2)
    compute(0, 44, 2)
    sixes(1, 4, 5)
    for j in range(2):
        @pl.when(origins[j][0] != me_o)
        def _():
            hear(5 + j)
    arrived(46, 2, 10)
    compute(0, 46, 2)

    place_here = zh * 16 + me_o
    for j in range(2):
        if j == 1:
            sixes(1, 3, 4)
            sixes(1, 5, 8)
        for k in range(CAP):
            ebuf[j, k] = acc[j * CAP + k].astype(jnp.bfloat16)
        home = origins[j][0] == me_o

        def give(i, carry):
            a = (me_a + i) % 16
            src = ebuf.at[j, :, pl.ds(pl.multiple_of(a * ROWS, ROWS), ROWS), :]
            here = jnp.logical_and(home, i == 0)

            @pl.when(jnp.logical_not(here))
            def _():
                pltpu.make_async_remote_copy(
                    src_ref=src, dst_ref=erecv.at[place_here], send_sem=esend.at[j], recv_sem=erecv_sem,
                    device_id=(origins[j][0], a), device_id_type=MESH,
                ).start()

            @pl.when(here)
            def _():
                pltpu.make_async_copy(src, erecv.at[place_here], erecv_sem).start()

            return carry

        lax.fori_loop(0, 16, give, 0)

    def sent(ref, sem):
        pltpu.make_async_copy(ref, ref, sem).wait()

    sent(fbuf.at[pl.ds(0, 42)], fsend)
    for j in range(2):
        @pl.when(targets[j][0] != me_o)
        def _():
            sent(packed.at[j], asend.at[j])

    pltpu.make_async_copy(erecv, erecv, erecv_sem).wait()

    live = count[me_o]

    def unpack(p, carry):
        d, k = jnp.clip(domain[p], 0, 15), jnp.minimum(rank[p], CAP - 1)
        term = erecv[d, k].astype(jnp.float32) + erecv[16 + d, k].astype(jnp.float32)
        out[p] = jnp.where(p < live, term, 0.0)
        return carry

    lax.fori_loop(0, 32, unpack, 0)

    for j in range(2):
        @pl.when(origins[j][0] != me_o)
        def _():
            sent(ebuf.at[j], esend.at[j])

        @pl.when(origins[j][0] == me_o)
        def _():
            sent(ebuf.at[j, :, pl.ds(0, 15 * ROWS), :], esend.at[j])


def per_device(factor, amplitudes, pair_domain, pair_count):
    hbm = pl.BlockSpec(memory_space=pl.ANY)
    square = (256, 256)
    return pl.pallas_call(
        kernel,
        out_shape=jax.ShapeDtypeStruct((32, ROWS, 256), jnp.float32),
        in_specs=[hbm, hbm, hbm, hbm],
        out_specs=pl.BlockSpec(memory_space=pltpu.VMEM),
        scratch_shapes=[
            pltpu.VMEM((48,) + square, jnp.bfloat16),
            pltpu.VMEM((32,) + square, jnp.bfloat16),
            pltpu.VMEM((2, CAP) + square, jnp.bfloat16),
            pltpu.VMEM((SLOTS,) + square, jnp.bfloat16),
            pltpu.VMEM((SLOTS,) + square, jnp.float32),
            pltpu.VMEM((2, CAP) + square, jnp.bfloat16),
            pltpu.VMEM((32, CAP, ROWS, 256), jnp.bfloat16),
            pltpu.SMEM((32,), jnp.int32),
            pltpu.SMEM((16,), jnp.int32),
            pltpu.SMEM((32,), jnp.int32),
            pltpu.SemaphoreType.DMA,
            pltpu.SemaphoreType.DMA((11,)),
            pltpu.SemaphoreType.DMA((2,)),
            pltpu.SemaphoreType.DMA((2,)),
            pltpu.SemaphoreType.DMA((2,)),
            pltpu.SemaphoreType.DMA,
            pltpu.SemaphoreType.DMA((4,)),
            pltpu.SemaphoreType.REGULAR((7,)),
        ],
        compiler_params=pltpu.CompilerParams(
            collective_id=0, has_side_effects=True, vmem_limit_bytes=64 * 2**20 - 2**16
        ),
        cost_estimate=pl.CostEstimate(flops=20 * 10**9, bytes_accessed=6 * 10**6, transcendentals=0),
    )(factor.reshape(6, 256, 256), amplitudes, pair_domain, pair_count)


def solution(mesh):
    placed = (P("occ", "aux", None, None), P("occ", None, None), P("occ"), P())
    return jax.shard_map(
        per_device, mesh=mesh, in_specs=placed, out_specs=P("occ", "aux", None), check_vma=False
    )
```

```python
import jax
import jax.numpy as jnp
from jax import lax
from jax.experimental import pallas as pl
from jax.experimental.pallas import tpu as pltpu
from jax.sharding import PartitionSpec as P

MESH = pl.DeviceIdType.MESH
NT = (((1,), (1,)), ((), ()))
CAP = 3
SLOTS = 2 * CAP
ROWS = 16


def kernel(
    factor, amps, domain_hbm, count_hbm, out,
    fbuf, ampv, packed, arecv, acc, ebuf, erecv, domain, count, rank,
    fsend, frecv, asend, arecv_sem, esend, erecv_sem, local_sem, ready,
):
    me_o, me_a = lax.axis_index("occ"), lax.axis_index("aux")
    z, x = me_o // 4, me_o % 4
    y, zh, core = me_a // 4, (me_a // 2) % 2, me_a % 2
    up = ((y + 1) % 4) * 4 + me_a % 4
    down = ((y + 3) % 4) * 4 + me_a % 4
    sibling = me_a + 1 - 2 * core
    partner = me_a + 2 - 4 * zh
    z8 = zh * 4 + z

    def steps(j, h=0):
        dz = 1 - j + 2 * core
        ring = dz * (1 + 2 * h) if j else dz + 4 * core
        return (dz + 4 - y) % 4, ring

    def ahead(j, h=0):
        dx, ring = steps(j, h)
        to = (z8 + ring) % 8
        return (to % 4) * 4 + (x + dx) % 4, (y * 2 + to // 4) * 2 + core

    def behind(j, h=0):
        dx, ring = steps(j, h)
        to = (z8 + 8 - ring) % 8
        return (to % 4) * 4 + (x + 4 - dx) % 4, (y * 2 + to // 4) * 2 + core

    get_factor = pltpu.make_async_copy(factor, fbuf.at[pl.ds(0, 6)], local_sem.at[0])
    get_amps = pltpu.make_async_copy(amps, ampv, local_sem.at[1])
    get_domain = pltpu.make_async_copy(domain_hbm, domain, local_sem.at[2])
    get_count = pltpu.make_async_copy(count_hbm, count, local_sem.at[3])
    get_domain.start()
    get_factor.start()
    get_amps.start()
    get_count.start()

    barrier = pltpu.get_barrier_semaphore()
    for peer in (up, down, sibling, partner):
        pl.semaphore_signal(barrier, inc=1, device_id=(me_o, peer), device_id_type=MESH)
    targets = [ahead(j) for j in range(2)]
    origins = [behind(j) for j in range(2)]
    for j in range(2):
        src = origins[j]

        @pl.when(src[0] != me_o)
        def _():
            pl.semaphore_signal(barrier, inc=1, device_id=src, device_id_type=MESH)

    @pl.when(core == 1)
    def _():
        pl.semaphore_signal(barrier, inc=1, device_id=behind(1, 1), device_id_type=MESH)

    at_home = jnp.where(jnp.logical_and(y == 0, core == 0), 1, 0)
    pl.semaphore_wait(barrier, 6 + core - at_home)

    def fcopy(src, dst, size, n, peer):
        return pltpu.make_async_remote_copy(
            src_ref=fbuf.at[pl.ds(src, size)], dst_ref=fbuf.at[pl.ds(dst, size)],
            send_sem=fsend, recv_sem=frecv.at[n], device_id=(me_o, peer), device_id_type=MESH,
        )

    def arrived(first, size, n):
        ref = fbuf.at[pl.ds(first, size)]
        pltpu.make_async_copy(ref, ref, frecv.at[n]).wait()

    get_factor.wait()
    fcopy(0, 12, 3, 0, up).start()
    fcopy(3, 15, 3, 0, down).start()
    fcopy(0, 6, 6, 1, sibling).start()

    def find(p, carry):
        own = domain[p]
        new = []
        for j in range(2):
            seen, picks = carry[j]
            hit = own == targets[j][0]
            picks = tuple(jnp.where(jnp.logical_and(hit, seen == k), p, picks[k]) for k in range(CAP))
            new.append((seen + jnp.where(hit, 1, 0), picks))
        return tuple(new)

    get_domain.wait()
    zero = jnp.int32(0)
    start = (zero, (zero, zero, zero))
    found = lax.fori_loop(0, 32, find, (start, start))
    get_amps.wait()

    def pack(j):
        for k in range(CAP):
            packed[j, k] = ampv[found[j][1][k]]

    def amps_go(j):
        for k in range(CAP):
            for h in range(2):
                half = pl.ds(128 * h, 128)
                src, dst = packed.at[j, k, half, :], arecv.at[j * CAP + k, half, :]

                @pl.when(targets[j][0] != me_o)
                def _():
                    pltpu.make_async_remote_copy(
                        src_ref=src, dst_ref=dst, send_sem=asend.at[j], recv_sem=arecv_sem.at[j],
                        device_id=ahead(j, h), device_id_type=MESH,
                    ).start()

                @pl.when(targets[j][0] == me_o)
                def _():
                    pltpu.make_async_copy(src, dst, arecv_sem.at[j]).start()

    pack(0)
    amps_go(0)
    pack(1)
    fcopy(3, 24, 3, 2, up).start()
    fcopy(0, 27, 3, 2, down).start()

    def amps_arrive(j):
        ref = arecv.at[pl.ds(j * CAP, CAP)]
        pltpu.make_async_copy(ref, ref, arecv_sem.at[j]).wait()

    def tell(n, device):
        pl.semaphore_signal(ready.at[n], inc=1, device_id=device, device_id_type=MESH)

    def hear(n):
        pl.semaphore_wait(ready.at[n], 1)

    tell(0, (me_o, sibling))

    def place(p, carry):
        own = domain[p]
        before = zero
        for q in range(31):
            before += jnp.where(jnp.logical_and(domain[q] == own, q < p), 1, 0)
        rank[p] = before
        return carry

    lax.fori_loop(0, 32, place, 0)
    get_count.wait()
    hear(0)
    tell(1, (me_o, partner))
    acc[...] = jnp.zeros(acc.shape, jnp.float32)
    hear(1)
    tell(2, (me_o, up))
    tell(3, (me_o, down))

    def compute(j, first, size):
        b = fbuf[pl.ds(first, size)]
        tall = b.reshape(size * 256, 256)
        wide = jnp.concatenate([b[q] for q in range(size)], axis=1)
        for s in range(j * CAP, (j + 1) * CAP):
            half = jnp.dot(tall, arecv[s], preferred_element_type=jnp.float32).astype(jnp.bfloat16)
            half = jnp.concatenate([half[q * 256:(q + 1) * 256] for q in range(size)], axis=1)
            acc[s] += lax.dot_general(half, wide, NT, preferred_element_type=jnp.float32)

    def sixes(j, first, stop):
        def body(i, carry):
            compute(j, 6 * i, 6)
            return carry

        lax.fori_loop(first, stop, body, 0)

    def relay(g):
        arrived(36 + 4 * g, 2, 3 + g)
        fcopy(36 + 4 * g, 38 + 4 * g, 2, 8 + g, sibling).start()

    arrived(6, 6, 1)
    amps_arrive(0)
    amps_go(1)
    sixes(0, 0, 2)
    arrived(12, 6, 0)
    for g in range(3):
        fcopy(12 + g, 36 + 4 * g, 1, 3 + g, up).start()
        fcopy(15 + g, 37 + 4 * g, 1, 3 + g, down).start()
    fcopy(12, 18, 6, 6, sibling).start()
    hear(2)
    hear(3)
    tell(4, (me_o, up))
    sixes(0, 2, 3)
    arrived(18, 6, 6)
    sixes(0, 3, 4)
    hear(4)
    for j in range(2):
        @pl.when(targets[j][0] != me_o)
        def _():
            tell(5 + j, targets[j])

    amps_arrive(1)
    sixes(1, 0, 2)
    arrived(24, 6, 2)
    fcopy(24, 30, 6, 7, sibling).start()
    sixes(0, 4, 5)
    arrived(30, 6, 7)
    sixes(0, 5, 6)
    relay(0)
    arrived(38, 2, 8)
    compute(0, 36, 4)
    relay(1)
    arrived(42, 2, 9)
    compute(0, 40, 4)
    relay(2)
    compute(0, 44, 2)
    sixes(1, 4, 5)
    for j in range(2):
        @pl.when(origins[j][0] != me_o)
        def _():
            hear(5 + j)
    arrived(46, 2, 10)
    compute(0, 46, 2)

    place_here = zh * 16 + me_o
    for j in range(2):
        if j == 1:
            sixes(1, 2, 4)
            sixes(1, 5, 8)
        for k in range(CAP):
            ebuf[j, k] = acc[j * CAP + k].astype(jnp.bfloat16)
        home = origins[j][0] == me_o

        def give(i, carry):
            a = (me_a + i) % 16
            src = ebuf.at[j, :, pl.ds(pl.multiple_of(a * ROWS, ROWS), ROWS), :]
            here = jnp.logical_and(home, i == 0)

            @pl.when(jnp.logical_not(here))
            def _():
                pltpu.make_async_remote_copy(
                    src_ref=src, dst_ref=erecv.at[place_here], send_sem=esend.at[j], recv_sem=erecv_sem,
                    device_id=(origins[j][0], a), device_id_type=MESH,
                ).start()

            @pl.when(here)
            def _():
                pltpu.make_async_copy(src, erecv.at[place_here], erecv_sem).start()

            return carry

        lax.fori_loop(0, 16, give, 0)

    def sent(ref, sem):
        pltpu.make_async_copy(ref, ref, sem).wait()

    sent(fbuf.at[pl.ds(0, 42)], fsend)
    for j in range(2):
        @pl.when(targets[j][0] != me_o)
        def _():
            sent(packed.at[j], asend.at[j])

    pltpu.make_async_copy(erecv, erecv, erecv_sem).wait()

    live = count[me_o]

    def unpack(p, carry):
        d, k = jnp.clip(domain[p], 0, 15), jnp.minimum(rank[p], CAP - 1)
        term = erecv[d, k].astype(jnp.float32) + erecv[16 + d, k].astype(jnp.float32)
        out[p] = jnp.where(p < live, term, 0.0)
        return carry

    lax.fori_loop(0, 32, unpack, 0)

    for j in range(2):
        @pl.when(origins[j][0] != me_o)
        def _():
            sent(ebuf.at[j], esend.at[j])

        @pl.when(origins[j][0] == me_o)
        def _():
            sent(ebuf.at[j, :, pl.ds(0, 15 * ROWS), :], esend.at[j])


def per_device(factor, amplitudes, pair_domain, pair_count):
    hbm = pl.BlockSpec(memory_space=pl.ANY)
    square = (256, 256)
    return pl.pallas_call(
        kernel,
        out_shape=jax.ShapeDtypeStruct((32, ROWS, 256), jnp.float32),
        in_specs=[hbm, hbm, hbm, hbm],
        out_specs=pl.BlockSpec(memory_space=pltpu.VMEM),
        scratch_shapes=[
            pltpu.VMEM((48,) + square, jnp.bfloat16),
            pltpu.VMEM((32,) + square, jnp.bfloat16),
            pltpu.VMEM((2, CAP) + square, jnp.bfloat16),
            pltpu.VMEM((SLOTS,) + square, jnp.bfloat16),
            pltpu.VMEM((SLOTS,) + square, jnp.float32),
            pltpu.VMEM((2, CAP) + square, jnp.bfloat16),
            pltpu.VMEM((32, CAP, ROWS, 256), jnp.bfloat16),
            pltpu.SMEM((32,), jnp.int32),
            pltpu.SMEM((16,), jnp.int32),
            pltpu.SMEM((32,), jnp.int32),
            pltpu.SemaphoreType.DMA,
            pltpu.SemaphoreType.DMA((11,)),
            pltpu.SemaphoreType.DMA((2,)),
            pltpu.SemaphoreType.DMA((2,)),
            pltpu.SemaphoreType.DMA((2,)),
            pltpu.SemaphoreType.DMA,
            pltpu.SemaphoreType.DMA((4,)),
            pltpu.SemaphoreType.REGULAR((7,)),
        ],
        compiler_params=pltpu.CompilerParams(
            collective_id=0, has_side_effects=True, vmem_limit_bytes=64 * 2**20 - 2**16
        ),
        cost_estimate=pl.CostEstimate(flops=20 * 10**9, bytes_accessed=6 * 10**6, transcendentals=0),
    )(factor.reshape(6, 256, 256), amplitudes, pair_domain, pair_count)


def solution(mesh):
    placed = (P("occ", "aux", None, None), P("occ", None, None), P("occ"), P())
    return jax.shard_map(
        per_device, mesh=mesh, in_specs=placed, out_specs=P("occ", "aux", None), check_vma=False
    )
```

```python
import jax
import jax.numpy as jnp
from jax import lax
from jax.experimental import pallas as pl
from jax.experimental.pallas import tpu as pltpu
from jax.sharding import PartitionSpec as P

MESH = pl.DeviceIdType.MESH
NT = (((1,), (1,)), ((), ()))
CAP = 3
SLOTS = 2 * CAP
ROWS = 16


def kernel(
    factor, amps, domain_hbm, count_hbm, out,
    fbuf, ampv, packed, arecv, acc, ebuf, erecv, domain, count, rank,
    fsend, frecv, asend, arecv_sem, esend, erecv_sem, local_sem, ready,
):
    me_o, me_a = lax.axis_index("occ"), lax.axis_index("aux")
    z, x = me_o // 4, me_o % 4
    y, zh, core = me_a // 4, (me_a // 2) % 2, me_a % 2
    up = ((y + 1) % 4) * 4 + me_a % 4
    down = ((y + 3) % 4) * 4 + me_a % 4
    sibling = me_a + 1 - 2 * core
    partner = me_a + 2 - 4 * zh
    z8 = zh * 4 + z

    def steps(j, h=0):
        dz = 1 - j + 2 * core
        ring = dz * (1 + 2 * h) if j else dz + 4 * core
        return (dz + 4 - y) % 4, ring

    def ahead(j, h=0):
        dx, ring = steps(j, h)
        to = (z8 + ring) % 8
        return (to % 4) * 4 + (x + dx) % 4, (y * 2 + to // 4) * 2 + core

    def behind(j, h=0):
        dx, ring = steps(j, h)
        to = (z8 + 8 - ring) % 8
        return (to % 4) * 4 + (x + 4 - dx) % 4, (y * 2 + to // 4) * 2 + core

    get_factor = pltpu.make_async_copy(factor, fbuf.at[pl.ds(0, 6)], local_sem.at[0])
    get_amps = pltpu.make_async_copy(amps, ampv, local_sem.at[1])
    get_domain = pltpu.make_async_copy(domain_hbm, domain, local_sem.at[2])
    get_count = pltpu.make_async_copy(count_hbm, count, local_sem.at[3])
    get_domain.start()
    get_factor.start()
    get_amps.start()
    get_count.start()

    barrier = pltpu.get_barrier_semaphore()
    for peer in (up, down, sibling, partner):
        pl.semaphore_signal(barrier, inc=1, device_id=(me_o, peer), device_id_type=MESH)
    targets = [ahead(j) for j in range(2)]
    origins = [behind(j) for j in range(2)]
    for j in range(2):
        src = origins[j]

        @pl.when(src[0] != me_o)
        def _():
            pl.semaphore_signal(barrier, inc=1, device_id=src, device_id_type=MESH)

    @pl.when(core == 1)
    def _():
        pl.semaphore_signal(barrier, inc=1, device_id=behind(1, 1), device_id_type=MESH)

    at_home = jnp.where(jnp.logical_and(y == 0, core == 0), 1, 0)
    pl.semaphore_wait(barrier, 6 + core - at_home)

    def fcopy(src, dst, size, n, peer):
        return pltpu.make_async_remote_copy(
            src_ref=fbuf.at[pl.ds(src, size)], dst_ref=fbuf.at[pl.ds(dst, size)],
            send_sem=fsend, recv_sem=frecv.at[n], device_id=(me_o, peer), device_id_type=MESH,
        )

    def arrived(first, size, n):
        ref = fbuf.at[pl.ds(first, size)]
        pltpu.make_async_copy(ref, ref, frecv.at[n]).wait()

    get_factor.wait()
    fcopy(0, 12, 3, 0, up).start()
    fcopy(3, 15, 3, 0, down).start()
    fcopy(0, 6, 6, 1, sibling).start()

    def find(p, carry):
        own = domain[p]
        new = []
        for j in range(2):
            seen, picks = carry[j]
            hit = own == targets[j][0]
            picks = tuple(jnp.where(jnp.logical_and(hit, seen == k), p, picks[k]) for k in range(CAP))
            new.append((seen + jnp.where(hit, 1, 0), picks))
        return tuple(new)

    get_domain.wait()
    zero = jnp.int32(0)
    start = (zero, (zero, zero, zero))
    found = lax.fori_loop(0, 32, find, (start, start))
    get_amps.wait()

    def pack(j):
        for k in range(CAP):
            packed[j, k] = ampv[found[j][1][k]]

    def amps_go(j):
        for k in range(CAP):
            for h in range(2):
                half = pl.ds(128 * h, 128)
                src, dst = packed.at[j, k, half, :], arecv.at[j * CAP + k, half, :]

                @pl.when(targets[j][0] != me_o)
                def _():
                    pltpu.make_async_remote_copy(
                        src_ref=src, dst_ref=dst, send_sem=asend.at[j], recv_sem=arecv_sem.at[j],
                        device_id=ahead(j, h), device_id_type=MESH,
                    ).start()

                @pl.when(targets[j][0] == me_o)
                def _():
                    pltpu.make_async_copy(src, dst, arecv_sem.at[j]).start()

    pack(0)
    amps_go(0)
    pack(1)
    fcopy(3, 24, 3, 2, up).start()
    fcopy(0, 27, 3, 2, down).start()

    def amps_arrive(j):
        ref = arecv.at[pl.ds(j * CAP, CAP)]
        pltpu.make_async_copy(ref, ref, arecv_sem.at[j]).wait()

    def tell(n, device):
        pl.semaphore_signal(ready.at[n], inc=1, device_id=device, device_id_type=MESH)

    def hear(n):
        pl.semaphore_wait(ready.at[n], 1)

    tell(0, (me_o, sibling))

    hear(0)
    tell(1, (me_o, partner))
    acc[...] = jnp.zeros(acc.shape, jnp.float32)

    def compute(j, first, size):
        b = fbuf[pl.ds(first, size)]
        tall = b.reshape(size * 256, 256)
        wide = jnp.concatenate([b[q] for q in range(size)], axis=1)
        for s in range(j * CAP, (j + 1) * CAP):
            half = jnp.dot(tall, arecv[s], preferred_element_type=jnp.float32).astype(jnp.bfloat16)
            half = jnp.concatenate([half[q * 256:(q + 1) * 256] for q in range(size)], axis=1)
            acc[s] += lax.dot_general(half, wide, NT, preferred_element_type=jnp.float32)

    def sixes(j, first, stop):
        def body(i, carry):
            compute(j, 6 * i, 6)
            return carry

        lax.fori_loop(first, stop, body, 0)

    def relay(g):
        arrived(36 + 4 * g, 2, 3 + g)
        fcopy(36 + 4 * g, 38 + 4 * g, 2, 8 + g, sibling).start()

    arrived(6, 6, 1)
    amps_arrive(0)
    amps_go(1)
    hear(1)
    tell(2, (me_o, up))
    tell(3, (me_o, down))
    sixes(0, 0, 2)
    arrived(12, 6, 0)
    for g in range(3):
        fcopy(12 + g, 36 + 4 * g, 1, 3 + g, up).start()
        fcopy(15 + g, 37 + 4 * g, 1, 3 + g, down).start()
    fcopy(12, 18, 6, 6, sibling).start()
    hear(2)
    hear(3)
    tell(4, (me_o, up))
    sixes(0, 2, 3)
    arrived(18, 6, 6)
    sixes(0, 3, 4)
    hear(4)
    for j in range(2):
        @pl.when(targets[j][0] != me_o)
        def _():
            tell(5 + j, targets[j])

    amps_arrive(1)
    sixes(1, 0, 2)
    arrived(24, 6, 2)
    fcopy(24, 30, 6, 7, sibling).start()
    sixes(0, 4, 5)
    arrived(30, 6, 7)
    sixes(0, 5, 6)
    relay(0)
    sixes(1, 2, 3)
    arrived(38, 2, 8)
    compute(0, 36, 4)
    relay(1)
    arrived(42, 2, 9)
    compute(0, 40, 4)
    relay(2)
    compute(0, 44, 2)
    sixes(1, 4, 5)
    for j in range(2):
        @pl.when(origins[j][0] != me_o)
        def _():
            hear(5 + j)
    arrived(46, 2, 10)
    compute(0, 46, 2)

    place_here = zh * 16 + me_o
    for j in range(2):
        if j == 1:
            sixes(1, 3, 4)
            sixes(1, 5, 8)
        for k in range(CAP):
            ebuf[j, k] = acc[j * CAP + k].astype(jnp.bfloat16)
        home = origins[j][0] == me_o

        def give(i, carry):
            a = (me_a + i) % 16
            src = ebuf.at[j, :, pl.ds(pl.multiple_of(a * ROWS, ROWS), ROWS), :]
            here = jnp.logical_and(home, i == 0)

            @pl.when(jnp.logical_not(here))
            def _():
                pltpu.make_async_remote_copy(
                    src_ref=src, dst_ref=erecv.at[place_here], send_sem=esend.at[j], recv_sem=erecv_sem,
                    device_id=(origins[j][0], a), device_id_type=MESH,
                ).start()

            @pl.when(here)
            def _():
                pltpu.make_async_copy(src, erecv.at[place_here], erecv_sem).start()

            return carry

        lax.fori_loop(0, 16, give, 0)

    def place(p, carry):
        own = domain[p]
        before = zero
        for q in range(31):
            before += jnp.where(jnp.logical_and(domain[q] == own, q < p), 1, 0)
        rank[p] = before
        return carry

    lax.fori_loop(0, 32, place, 0)
    get_count.wait()
    def sent(ref, sem):
        pltpu.make_async_copy(ref, ref, sem).wait()

    sent(fbuf.at[pl.ds(0, 42)], fsend)
    for j in range(2):
        @pl.when(targets[j][0] != me_o)
        def _():
            sent(packed.at[j], asend.at[j])

    pltpu.make_async_copy(erecv, erecv, erecv_sem).wait()

    live = count[me_o]

    def unpack(p, carry):
        d, k = jnp.clip(domain[p], 0, 15), jnp.minimum(rank[p], CAP - 1)
        term = erecv[d, k].astype(jnp.float32) + erecv[16 + d, k].astype(jnp.float32)
        out[p] = jnp.where(p < live, term, 0.0)
        return carry

    lax.fori_loop(0, 32, unpack, 0)

    for j in range(2):
        @pl.when(origins[j][0] != me_o)
        def _():
            sent(ebuf.at[j], esend.at[j])

        @pl.when(origins[j][0] == me_o)
        def _():
            sent(ebuf.at[j, :, pl.ds(0, 15 * ROWS), :], esend.at[j])


def per_device(factor, amplitudes, pair_domain, pair_count):
    hbm = pl.BlockSpec(memory_space=pl.ANY)
    square = (256, 256)
    return pl.pallas_call(
        kernel,
        out_shape=jax.ShapeDtypeStruct((32, ROWS, 256), jnp.float32),
        in_specs=[hbm, hbm, hbm, hbm],
        out_specs=pl.BlockSpec(memory_space=pltpu.VMEM),
        scratch_shapes=[
            pltpu.VMEM((48,) + square, jnp.bfloat16),
            pltpu.VMEM((32,) + square, jnp.bfloat16),
            pltpu.VMEM((2, CAP) + square, jnp.bfloat16),
            pltpu.VMEM((SLOTS,) + square, jnp.bfloat16),
            pltpu.VMEM((SLOTS,) + square, jnp.float32),
            pltpu.VMEM((2, CAP) + square, jnp.bfloat16),
            pltpu.VMEM((32, CAP, ROWS, 256), jnp.bfloat16),
            pltpu.SMEM((32,), jnp.int32),
            pltpu.SMEM((16,), jnp.int32),
            pltpu.SMEM((32,), jnp.int32),
            pltpu.SemaphoreType.DMA,
            pltpu.SemaphoreType.DMA((11,)),
            pltpu.SemaphoreType.DMA((2,)),
            pltpu.SemaphoreType.DMA((2,)),
            pltpu.SemaphoreType.DMA((2,)),
            pltpu.SemaphoreType.DMA,
            pltpu.SemaphoreType.DMA((4,)),
            pltpu.SemaphoreType.REGULAR((7,)),
        ],
        compiler_params=pltpu.CompilerParams(
            collective_id=0, has_side_effects=True, vmem_limit_bytes=64 * 2**20 - 2**16
        ),
        cost_estimate=pl.CostEstimate(flops=20 * 10**9, bytes_accessed=6 * 10**6, transcendentals=0),
    )(factor.reshape(6, 256, 256), amplitudes, pair_domain, pair_count)


def solution(mesh):
    placed = (P("occ", "aux", None, None), P("occ", None, None), P("occ"), P())
    return jax.shard_map(
        per_device, mesh=mesh, in_specs=placed, out_specs=P("occ", "aux", None), check_vma=False
    )
```

```python
import jax
import jax.numpy as jnp
from jax import lax
from jax.experimental import pallas as pl
from jax.experimental.pallas import tpu as pltpu
from jax.sharding import PartitionSpec as P

MESH = pl.DeviceIdType.MESH
NT = (((1,), (1,)), ((), ()))
CAP = 3
SLOTS = 2 * CAP
ROWS = 16


def kernel(
    factor, amps, domain_hbm, count_hbm, out,
    fbuf, ampv, packed, arecv, acc, ebuf, erecv, domain, count, rank,
    fsend, frecv, asend, arecv_sem, esend, erecv_sem, local_sem, ready,
):
    me_o, me_a = lax.axis_index("occ"), lax.axis_index("aux")
    z, x = me_o // 4, me_o % 4
    y, zh, core = me_a // 4, (me_a // 2) % 2, me_a % 2
    up = ((y + 1) % 4) * 4 + me_a % 4
    down = ((y + 3) % 4) * 4 + me_a % 4
    sibling = me_a + 1 - 2 * core
    partner = me_a + 2 - 4 * zh
    z8 = zh * 4 + z

    def steps(j, h=0):
        dz = 1 - j + 2 * core
        ring = dz * (1 + 2 * h) if j else dz + 4 * core
        return (dz + 4 - y) % 4, ring

    def ahead(j, h=0):
        dx, ring = steps(j, h)
        to = (z8 + ring) % 8
        return (to % 4) * 4 + (x + dx) % 4, (y * 2 + to // 4) * 2 + core

    def behind(j, h=0):
        dx, ring = steps(j, h)
        to = (z8 + 8 - ring) % 8
        return (to % 4) * 4 + (x + 4 - dx) % 4, (y * 2 + to // 4) * 2 + core

    get_factor = pltpu.make_async_copy(factor, fbuf.at[pl.ds(0, 6)], local_sem.at[0])
    get_amps = pltpu.make_async_copy(amps, ampv, local_sem.at[1])
    get_domain = pltpu.make_async_copy(domain_hbm, domain, local_sem.at[2])
    get_count = pltpu.make_async_copy(count_hbm, count, local_sem.at[3])
    get_domain.start()
    get_factor.start()
    get_amps.start()
    get_count.start()

    barrier = pltpu.get_barrier_semaphore()
    for peer in (up, down, sibling, partner):
        pl.semaphore_signal(barrier, inc=1, device_id=(me_o, peer), device_id_type=MESH)
    targets = [ahead(j) for j in range(2)]
    origins = [behind(j) for j in range(2)]
    for j in range(2):
        src = origins[j]

        @pl.when(src[0] != me_o)
        def _():
            pl.semaphore_signal(barrier, inc=1, device_id=src, device_id_type=MESH)

    @pl.when(core == 1)
    def _():
        pl.semaphore_signal(barrier, inc=1, device_id=behind(1, 1), device_id_type=MESH)

    at_home = jnp.where(jnp.logical_and(y == 0, core == 0), 1, 0)
    pl.semaphore_wait(barrier, 6 + core - at_home)

    def fcopy(src, dst, size, n, peer):
        return pltpu.make_async_remote_copy(
            src_ref=fbuf.at[pl.ds(src, size)], dst_ref=fbuf.at[pl.ds(dst, size)],
            send_sem=fsend, recv_sem=frecv.at[n], device_id=(me_o, peer), device_id_type=MESH,
        )

    def arrived(first, size, n):
        ref = fbuf.at[pl.ds(first, size)]
        pltpu.make_async_copy(ref, ref, frecv.at[n]).wait()

    get_factor.wait()
    fcopy(0, 12, 3, 0, up).start()
    fcopy(3, 15, 3, 0, down).start()
    fcopy(0, 6, 6, 1, sibling).start()

    def find(p, carry):
        own = domain[p]
        new = []
        for j in range(2):
            seen, picks = carry[j]
            hit = own == targets[j][0]
            picks = tuple(jnp.where(jnp.logical_and(hit, seen == k), p, picks[k]) for k in range(CAP))
            new.append((seen + jnp.where(hit, 1, 0), picks))
        return tuple(new)

    get_domain.wait()
    zero = jnp.int32(0)
    start = (zero, (zero, zero, zero))
    found = lax.fori_loop(0, 32, find, (start, start))
    get_amps.wait()

    def pack(j):
        for k in range(CAP):
            packed[j, k] = ampv[found[j][1][k]]

    def amps_go(j):
        for k in range(CAP):
            for h in range(2):
                half = pl.ds(128 * h, 128)
                src, dst = packed.at[j, k, half, :], arecv.at[j * CAP + k, half, :]

                @pl.when(targets[j][0] != me_o)
                def _():
                    pltpu.make_async_remote_copy(
                        src_ref=src, dst_ref=dst, send_sem=asend.at[j], recv_sem=arecv_sem.at[j],
                        device_id=ahead(j, h), device_id_type=MESH,
                    ).start()

                @pl.when(targets[j][0] == me_o)
                def _():
                    pltpu.make_async_copy(src, dst, arecv_sem.at[j]).start()

    pack(0)
    amps_go(0)
    pack(1)
    fcopy(3, 24, 3, 2, up).start()
    fcopy(0, 27, 3, 2, down).start()

    def amps_arrive(j):
        ref = arecv.at[pl.ds(j * CAP, CAP)]
        pltpu.make_async_copy(ref, ref, arecv_sem.at[j]).wait()

    def tell(n, device):
        pl.semaphore_signal(ready.at[n], inc=1, device_id=device, device_id_type=MESH)

    def hear(n):
        pl.semaphore_wait(ready.at[n], 1)

    tell(0, (me_o, sibling))

    def place(p, carry):
        own = domain[p]
        before = zero
        for q in range(31):
            before += jnp.where(jnp.logical_and(domain[q] == own, q < p), 1, 0)
        rank[p] = before
        return carry

    lax.fori_loop(0, 32, place, 0)
    get_count.wait()
    hear(0)
    tell(1, (me_o, partner))
    acc[...] = jnp.zeros(acc.shape, jnp.float32)
    hear(1)
    tell(2, (me_o, up))
    tell(3, (me_o, down))

    def compute(j, first, size):
        b = fbuf[pl.ds(first, size)]
        tall = b.reshape(size * 256, 256)
        wide = jnp.concatenate([b[q] for q in range(size)], axis=1)
        for s in range(j * CAP, (j + 1) * CAP):
            half = jnp.dot(tall, arecv[s], preferred_element_type=jnp.float32).astype(jnp.bfloat16)
            half = jnp.concatenate([half[q * 256:(q + 1) * 256] for q in range(size)], axis=1)
            acc[s] += lax.dot_general(half, wide, NT, preferred_element_type=jnp.float32)

    def sixes(j, first, stop):
        def body(i, carry):
            compute(j, 6 * i, 6)
            return carry

        lax.fori_loop(first, stop, body, 0)

    def relay(g):
        arrived(36 + 4 * g, 2, 3 + g)
        fcopy(36 + 4 * g, 38 + 4 * g, 2, 8 + g, sibling).start()

    arrived(6, 6, 1)
    amps_arrive(0)
    amps_go(1)
    sixes(0, 0, 2)
    arrived(12, 6, 0)
    for g in range(3):
        fcopy(12 + g, 36 + 4 * g, 1, 3 + g, up).start()
        fcopy(15 + g, 37 + 4 * g, 1, 3 + g, down).start()
    fcopy(12, 18, 6, 6, sibling).start()
    hear(2)
    hear(3)
    tell(4, (me_o, up))
    sixes(0, 2, 3)
    arrived(18, 6, 6)
    sixes(0, 3, 4)
    hear(4)
    for j in range(2):
        @pl.when(targets[j][0] != me_o)
        def _():
            tell(5 + j, targets[j])

    amps_arrive(1)
    sixes(1, 0, 2)
    arrived(24, 6, 2)
    fcopy(24, 30, 6, 7, sibling).start()
    sixes(0, 4, 5)
    arrived(30, 6, 7)
    sixes(0, 5, 6)
    relay(0)
    sixes(1, 2, 3)
    arrived(38, 2, 8)
    compute(0, 36, 4)
    relay(1)
    arrived(42, 2, 9)
    compute(0, 40, 4)
    relay(2)
    compute(0, 44, 2)
    sixes(1, 4, 5)
    for j in range(2):
        @pl.when(origins[j][0] != me_o)
        def _():
            hear(5 + j)
    arrived(46, 2, 10)
    compute(0, 46, 2)

    place_here = zh * 16 + me_o
    for j in range(2):
        if j == 1:
            sixes(1, 3, 4)
            sixes(1, 5, 8)
        for k in range(CAP):
            ebuf[j, k] = acc[j * CAP + k].astype(jnp.bfloat16)
        home = origins[j][0] == me_o

        def give(i, carry):
            a = (me_a + 2 + i) % 16
            src = ebuf.at[j, :, pl.ds(pl.multiple_of(a * ROWS, ROWS), ROWS), :]
            here = jnp.logical_and(home, i == 14)

            @pl.when(jnp.logical_not(here))
            def _():
                pltpu.make_async_remote_copy(
                    src_ref=src, dst_ref=erecv.at[place_here], send_sem=esend.at[j], recv_sem=erecv_sem,
                    device_id=(origins[j][0], a), device_id_type=MESH,
                ).start()

            @pl.when(here)
            def _():
                pltpu.make_async_copy(src, erecv.at[place_here], erecv_sem).start()

            return carry

        lax.fori_loop(0, 16, give, 0)

    def sent(ref, sem):
        pltpu.make_async_copy(ref, ref, sem).wait()

    sent(fbuf.at[pl.ds(0, 42)], fsend)
    for j in range(2):
        @pl.when(targets[j][0] != me_o)
        def _():
            sent(packed.at[j], asend.at[j])

    pltpu.make_async_copy(erecv, erecv, erecv_sem).wait()

    live = count[me_o]

    def unpack(p, carry):
        d, k = jnp.clip(domain[p], 0, 15), jnp.minimum(rank[p], CAP - 1)
        term = erecv[d, k].astype(jnp.float32) + erecv[16 + d, k].astype(jnp.float32)
        out[p] = jnp.where(p < live, term, 0.0)
        return carry

    lax.fori_loop(0, 32, unpack, 0)

    for j in range(2):
        @pl.when(origins[j][0] != me_o)
        def _():
            sent(ebuf.at[j], esend.at[j])

        @pl.when(origins[j][0] == me_o)
        def _():
            sent(ebuf.at[j, :, pl.ds(0, 15 * ROWS), :], esend.at[j])


def per_device(factor, amplitudes, pair_domain, pair_count):
    hbm = pl.BlockSpec(memory_space=pl.ANY)
    square = (256, 256)
    return pl.pallas_call(
        kernel,
        out_shape=jax.ShapeDtypeStruct((32, ROWS, 256), jnp.float32),
        in_specs=[hbm, hbm, hbm, hbm],
        out_specs=pl.BlockSpec(memory_space=pltpu.VMEM),
        scratch_shapes=[
            pltpu.VMEM((48,) + square, jnp.bfloat16),
            pltpu.VMEM((32,) + square, jnp.bfloat16),
            pltpu.VMEM((2, CAP) + square, jnp.bfloat16),
            pltpu.VMEM((SLOTS,) + square, jnp.bfloat16),
            pltpu.VMEM((SLOTS,) + square, jnp.float32),
            pltpu.VMEM((2, CAP) + square, jnp.bfloat16),
            pltpu.VMEM((32, CAP, ROWS, 256), jnp.bfloat16),
            pltpu.SMEM((32,), jnp.int32),
            pltpu.SMEM((16,), jnp.int32),
            pltpu.SMEM((32,), jnp.int32),
            pltpu.SemaphoreType.DMA,
            pltpu.SemaphoreType.DMA((11,)),
            pltpu.SemaphoreType.DMA((2,)),
            pltpu.SemaphoreType.DMA((2,)),
            pltpu.SemaphoreType.DMA((2,)),
            pltpu.SemaphoreType.DMA,
            pltpu.SemaphoreType.DMA((4,)),
            pltpu.SemaphoreType.REGULAR((7,)),
        ],
        compiler_params=pltpu.CompilerParams(
            collective_id=0, has_side_effects=True, vmem_limit_bytes=64 * 2**20 - 2**16
        ),
        cost_estimate=pl.CostEstimate(flops=20 * 10**9, bytes_accessed=6 * 10**6, transcendentals=0),
    )(factor.reshape(6, 256, 256), amplitudes, pair_domain, pair_count)


def solution(mesh):
    placed = (P("occ", "aux", None, None), P("occ", None, None), P("occ"), P())
    return jax.shard_map(
        per_device, mesh=mesh, in_specs=placed, out_specs=P("occ", "aux", None), check_vma=False
    )
```
